256 devices in a mesh: chan: 64 (over x, z_hi, y), tile: 4 (over z_lo, core).
Axes of the slice: x: 4, y: 4, z: 8 (z_hi: 4, z_lo: 2; z = z_hi * 2 + z_lo), core: 2. Of those that a mesh axis runs over, the one named last changes fastest.
Arguments:
- cube: float32 [512, 512, 1024], P('chan', 'tile'), may hold values from -6 to 6
- residual_op: float32 [512, 512], replicated, may hold values from -0.25 to 0.25
- taper_x: float32 [512], P('tile'), may hold values from 0.2 to 1
- taper_y: float32 [1024], replicated, may hold values from 0.2 to 1
Outputs:
- spectrum: bfloat16 [2, 512, 512, 1024], P(None, 'chan', None, 'tile')
The draws below stay inside these ranges and needn't reach their ends.
All inputs are finite; a program needn't handle non-finite values.
Results may differ from the reference program's by a relative error of at most 0.0069.
Values may be sent and summed in bfloat16 or wider, within the bound.
A program may use at most 64 MiB of HBM per device.

```python
import math
import jax
import jax.numpy as jnp
from jax import lax

C = 512
NX = 512
NY = 1024


def steps_of(rng, extent, split, least, largest):
    def one(position, blocks):
        heights = jax.random.uniform(jax.random.fold_in(jax.random.fold_in(rng, 6), position), (blocks,), jnp.float32, least / len(split), largest / len(split))
        return jnp.repeat(jnp.exp(heights), extent[position] // blocks).reshape((-1,) + (1,) * (len(extent) - position - 1))

    level = one(*split[0])
    for cut in split[1:]:
        level = level * one(*cut)
    return level


def centred(key, dims, deviation, most, cuts=(), held_as=jnp.bfloat16):
    values = jax.random.normal(key, dims, jnp.float32) * deviation
    if len(cuts) > 0:
        values = steps_of(key, dims, cuts, -0.22, 0.18) * values
    return jnp.clip(values, min=-most, max=most).astype(held_as)


def setup_inputs(seed: int = 0) -> dict:
    key_of = jax.random.split(jax.random.key(seed), 5)
    return {
        "cube": centred(key_of[0], (C, NX, NY), 1.0, 6.0, ((0, 64), (1, 4)), jnp.float32),
        "residual_op": centred(key_of[1], (C, C), C ** -0.5, 0.25, (), jnp.float32),
        "taper_x": jnp.clip(0.2 + 0.8 * jax.random.uniform(key_of[2], (NX,), jnp.float32) ** steps_of(key_of[2], (NX,), ((0, 4),), -0.2, 0.2), 0.2, 1.0),
        "taper_y": jnp.clip(jax.random.uniform(key_of[3], (NY,), jnp.float32, 0.2, 1.0), 0.2, 1.0),
    }


def tables(count):
    index = jnp.arange(count, dtype=jnp.int32)
    product = index[:, None] * index[None, :] % count
    angle = 2.0 * math.pi / count * product.astype(jnp.float32)
    scale = 1.0 / math.sqrt(count)
    return ((jnp.cos(angle) * scale).astype(jnp.bfloat16), (-jnp.sin(angle) * scale).astype(jnp.bfloat16))

def reference(cube, residual_op, taper_x, taper_y):
    cos_y, msin_y = tables(NY)
    cos_x, msin_x = tables(NX)
    block = 16
    cos_yf = cos_y.astype(jnp.float32)
    msin_yf = msin_y.astype(jnp.float32)

    def rows_block(start):
        piece = lax.dynamic_slice_in_dim(cube, start, block, 1)
        resid = jnp.dot(residual_op, piece.reshape(C, block * NY), precision=lax.Precision.HIGHEST, preferred_element_type=jnp.float32)
        resid = resid.reshape(C, block, NY)
        tx = lax.dynamic_slice_in_dim(taper_x, start, block, 0)
        tapered = (resid * tx[None, :, None] * taper_y[None, None, :]).astype(jnp.bfloat16)
        flat = tapered.reshape(C * block, NY).astype(jnp.float32)
        row_re = jnp.dot(flat, cos_yf, preferred_element_type=jnp.float32).astype(jnp.bfloat16)
        row_im = jnp.dot(flat, msin_yf, preferred_element_type=jnp.float32).astype(jnp.bfloat16)
        return jnp.stack([row_re, row_im]).reshape(2, C, block, NY)
    starts = (jnp.arange(NX // block, dtype=jnp.int32) * block).astype(jnp.int32)
    rows = lax.map(rows_block, starts)
    rows = jnp.transpose(rows, (1, 2, 0, 3, 4)).reshape(2, C, NX, NY)
    cos_xf = cos_x.astype(jnp.float32)
    msin_xf = msin_x.astype(jnp.float32)

    def one_channel(pair):
        real_part = pair[0].astype(jnp.float32)
        imag_part = pair[1].astype(jnp.float32)
        out_re = jnp.dot(cos_xf, real_part, preferred_element_type=jnp.float32) - jnp.dot(msin_xf, imag_part, preferred_element_type=jnp.float32)
        out_im = jnp.dot(cos_xf, imag_part, preferred_element_type=jnp.float32) + jnp.dot(msin_xf, real_part, preferred_element_type=jnp.float32)
        return jnp.stack([out_re, out_im]).astype(jnp.bfloat16)
    result = lax.map(one_channel, jnp.transpose(rows, (1, 0, 2, 3)))
    return jnp.transpose(result, (1, 0, 2, 3))
```

```python
import functools
import math

import jax
import jax.numpy as jnp
import ml_dtypes
import numpy as np
from jax import lax
from jax.experimental import pallas as pl
from jax.experimental.pallas import tpu as pltpu
from jax.sharding import PartitionSpec as P

MESH = pl.DeviceIdType.MESH
BF16 = jnp.bfloat16
F32 = jnp.float32
NX, NY = 512, 1024
PEERS = 63 + 32 + 2


def tables(count):
    index = np.arange(count, dtype=np.int64)
    angle = 2.0 * math.pi / count * ((index[:, None] * index[None, :]) % count)
    scale = 1.0 / math.sqrt(count)
    return (np.cos(angle) * scale).astype(np.float32), (-np.sin(angle) * scale).astype(np.float32)


def row_tables():
    cos_y, msin_y = tables(NY)
    parts = [np.concatenate([cos_y[:, 256 * t:256 * t + 256], msin_y[:, 256 * t:256 * t + 256]], 1) for t in range(4)]
    return np.stack(parts).astype(ml_dtypes.bfloat16)


def column_table():
    cos_x, msin_x = tables(NX)
    tile, zh, r, cx, cy = np.meshgrid(*[np.arange(n) for n in (4, 4, 2, 4, 4)], indexing="ij")
    order = (tile * 128 + r * 64 + cx * 16 + zh * 4 + cy).reshape(-1)
    cos_x, msin_x = cos_x[:, order], msin_x[:, order]
    whole = np.concatenate([np.concatenate([cos_x, -msin_x], 1), np.concatenate([msin_x, cos_x], 1)], 0)
    return whole.astype(ml_dtypes.bfloat16)


def mix_rows(cube, op, taper_x, taper_y, ytab, rows_out,
             held, sent, mixed_in, op2, tapered, land, table, wide, rows,
             cube_sem, table_sem, out_sem, send1, recv1, send2, land_sem,
             send_fwd, fwd_sem, send_sib, sib_sem, sibf_sem):
    c = lax.axis_index("chan")
    t = lax.axis_index("tile")
    x, j, y = c // 16, (c // 4) % 4, c % 4
    zl, co = t // 2, t % 2
    u = 1 - 2 * zl
    partner = (c, (1 - zl) * 2 + co)
    sibling = (c, zl * 2 + 1 - co)

    loads = [pltpu.make_async_copy(cube.at[:, pl.ds(128 * k, 128)], held.at[k], cube_sem.at[k]) for k in range(8)]
    for load in loads:
        load.start()
    table_load = pltpu.make_async_copy(ytab.at[t], table, table_sem)
    table_load.start()

    barrier = pltpu.get_barrier_semaphore()

    def greet(k, _):
        pl.semaphore_signal(barrier, inc=1, device_id=((c + k) % 64, t), device_id_type=MESH)
        return 0

    lax.fori_loop(1, 64, greet, 0)

    def greet_far(k, _):
        near = (j - u + 4) % 4
        far = (j + 2) % 4
        base = (k // 4) * 16 + k % 4
        for zh in (near, far):
            pl.semaphore_signal(barrier, inc=1, device_id=(base + zh * 4, (1 - zl) * 2 + co), device_id_type=MESH)
        return 0

    lax.fori_loop(0, 16, greet_far, 0)
    for other in (partner, sibling):
        pl.semaphore_signal(barrier, inc=1, device_id=other, device_id_type=MESH)

    for k in range(8):
        loads[k].wait()

        def cast(o, _, k=k):
            block = held[k, pl.ds(o, 16, stride=64), :]
            sent[pl.ds(pl.multiple_of(o * 16, 16), 16), 128 * k:128 * k + 128] = block.astype(BF16)
            return 0

        lax.fori_loop(0, 64, cast, 0, unroll=8)

    pl.semaphore_wait(barrier, PEERS)

    mine = pl.ds(pl.multiple_of(c * 16, 16), 16)
    own1 = pltpu.make_async_copy(sent.at[mine], mixed_in.at[mine], recv1)
    own1.start()

    def scatter(k, _):
        d = (c + k) % 64
        pltpu.make_async_remote_copy(
            src_ref=sent.at[pl.ds(pl.multiple_of(d * 16, 16), 16)], dst_ref=mixed_in.at[mine],
            send_sem=send1, recv_sem=recv1, device_id=(d, t), device_id_type=MESH).start()
        return 0

    lax.fori_loop(1, 64, scatter, 0)

    c2 = lax.broadcasted_iota(jnp.int32, (512, 1024), 0)
    spread_k = jnp.where(lax.broadcasted_iota(jnp.int32, (512, 1024), 1) // 2 == c2, 1.0, 0.0).astype(BF16)
    i = lax.broadcasted_iota(jnp.int32, (256, 512), 0)
    cc = lax.broadcasted_iota(jnp.int32, (256, 512), 1)
    same = (lax.broadcasted_iota(jnp.int32, (256, 1024), 0) % 2) == (lax.broadcasted_iota(jnp.int32, (256, 1024), 1) % 2)
    op_low = op[...].astype(BF16)

    def expand(zh, _):
        pick = jnp.where((i // 64) * 128 + zh * 32 + (i % 64) // 2 == cc, 1.0, 0.0).astype(BF16)
        some = jnp.dot(pick, op_low, preferred_element_type=F32).astype(BF16)
        full = jnp.dot(some, spread_k, preferred_element_type=F32)
        op2[pl.ds(pl.multiple_of(zh * 256, 256), 256), :] = jnp.where(same, full, 0.0).astype(BF16)
        return 0

    lax.fori_loop(0, 4, expand, 0)
    odd = lax.broadcasted_iota(jnp.int32, (256, 256), 0) % 2 == 1
    tx = jnp.where(odd, taper_x[0, c + 64], taper_x[0, c])
    table_load.wait()

    pltpu.make_async_copy(sent, mixed_in, recv1).wait()

    def mix(st, _):
        delta = jnp.where(st == 0, 0, jnp.where(st == 1, -u, jnp.where(st == 2, u, 2)))
        zh = (j + delta + 4) % 4
        start = pl.multiple_of(zh * 256, 256)

        def strip(n, _):
            cols = pl.ds(pl.multiple_of(n * 256, 256), 256)
            part = jnp.dot(op2[pl.ds(start, 256), :], mixed_in[:, cols], preferred_element_type=F32)
            tapered[pl.ds(start, 256), cols] = (part * tx * taper_y[:, cols]).astype(BF16)
            return 0

        lax.fori_loop(0, 4, strip, 0)
        far = st % 2
        to_tile = jnp.where(far == 1, (1 - zl) * 2 + co, t)

        def scatter2(k, _):
            dx = (x + k // 4) % 4
            dy = (y + k % 4) % 4
            src = tapered.at[pl.ds(pl.multiple_of(start + dx * 64 + dy * 16, 16), 16)]
            dst = land.at[t * 4 + j, pl.ds(pl.multiple_of(x * 64 + y * 16, 16), 16)]
            pltpu.make_async_remote_copy(
                src_ref=src, dst_ref=dst, send_sem=send2, recv_sem=land_sem.at[st * 4 + k // 4],
                device_id=(dx * 16 + zh * 4 + dy, to_tile), device_id_type=MESH).start()
            return 0

        first = jnp.where(st == 0, 1, 0)
        lax.fori_loop(first, 16, scatter2, 0)
        return 0

    lax.fori_loop(0, 4, mix, 0)
    own2 = pltpu.make_async_copy(
        tapered.at[pl.ds(pl.multiple_of(j * 256 + x * 64 + y * 16, 16), 16)],
        land.at[t * 4 + j, pl.ds(pl.multiple_of(x * 64 + y * 16, 16), 16)], land_sem.at[0])
    own2.start()

    def group_of(st, passed, other_core):
        z = zl + passed - 2 * zl * passed
        v = 1 - 2 * z
        h = (z + st) % 2
        zh = (j - jnp.where(st == 0, 0, jnp.where(st == 3, 2, v)) + 4) % 4
        core = co + other_core - 2 * co * other_core
        return (h * 2 + core) * 4 + zh

    def piece(st, e, passed, other_core):
        xs = (x - e + 4) % 4
        return land.at[group_of(st, passed, other_core), pl.ds(pl.multiple_of(xs * 64, 64), 64)]

    def arrived(ref, sem):
        pltpu.make_async_copy(ref, ref, sem).wait()

    def pass_on(ref, send, recv, device):
        pltpu.make_async_remote_copy(src_ref=ref, dst_ref=ref, send_sem=send, recv_sem=recv,
                                     device_id=device, device_id_type=MESH).start()

    def take_landed(n):
        st, e = n // 4, n % 4
        ref = piece(st, e, 0, 0)
        arrived(ref, land_sem.at[n])
        pass_on(ref, send_fwd, fwd_sem.at[n], partner)
        pass_on(ref, send_sib, sib_sem.at[n], sibling)

    def take_passed(n):
        st, e = n // 4, n % 4
        ref = piece(st, e, 1, 0)
        arrived(ref, fwd_sem.at[n])
        pass_on(ref, send_sib, sibf_sem.at[n], sibling)

    def take_sibling(st, passed, sem):
        for e in range(4):
            arrived(piece(st, e, passed, 1), sem.at[st * 4 + e])

    def transform(g):
        for n in range(2):
            part = jnp.dot(land[g], table[:, 256 * n:256 * n + 256], preferred_element_type=F32)
            wide[2 * n] = part[:, :128]
            wide[2 * n + 1] = part[:, 128:]
        for q in range(16):
            ch, r = q // 2, q % 2
            for n in range(4):
                at = pl.ds(pl.multiple_of(g * 32 + r * 16, 16), 16)
                rows[ch, n // 2, at, (n % 2) * 128:(n % 2) * 128 + 128] = wide[n, pl.ds(q, 16, stride=16), :].astype(BF16)
        span = pl.ds(pl.multiple_of(g * 32, 32), 32)
        pltpu.make_async_copy(rows.at[:, :, span], rows_out.at[:, :, span], out_sem).start()

    def first_pieces(n, _):
        take_landed(n)
        return 0

    lax.fori_loop(0, 4, first_pieces, 0)
    take_passed(0)
    take_passed(1)

    def stage(st, _):
        last = st - 1
        take_landed(st * 4)
        take_passed(st * 4 - 2)
        transform(group_of(last, 0, 0))
        take_landed(st * 4 + 1)
        take_passed(st * 4 - 1)
        take_sibling(last, 0, sib_sem)
        transform(group_of(last, 0, 1))
        take_landed(st * 4 + 2)
        take_passed(st * 4)
        transform(group_of(last, 1, 0))
        take_landed(st * 4 + 3)
        take_passed(st * 4 + 1)
        take_sibling(last, 1, sibf_sem)
        transform(group_of(last, 1, 1))
        return 0

    lax.fori_loop(1, 4, stage, 0)
    transform(group_of(3, 0, 0))
    take_passed(14)
    take_sibling(3, 0, sib_sem)
    transform(group_of(3, 0, 1))
    take_passed(15)
    transform(group_of(3, 1, 0))
    take_sibling(3, 1, sibf_sem)
    transform(group_of(3, 1, 1))

    pltpu.make_async_copy(rows, rows_out, out_sem).wait()
    less = pl.ds(0, 63 * 16)
    pltpu.make_async_copy(sent.at[less], mixed_in.at[less], send1).wait()
    pltpu.make_async_copy(tapered.at[less], tapered.at[less], send2).wait()
    pltpu.make_async_copy(land.at[pl.ds(0, 4)], land.at[pl.ds(0, 4)], send_fwd).wait()
    pltpu.make_async_copy(land.at[pl.ds(0, 8)], land.at[pl.ds(0, 8)], send_sib).wait()


def columns(table, rows, out):
    both = jnp.dot(table[...], rows[0], preferred_element_type=F32).astype(BF16)
    out[0, 0] = both[:512]
    out[1, 0] = both[512:]


def shards(cube, residual_op, taper_x, taper_y):
    vmem = pl.BlockSpec(memory_space=pltpu.VMEM)
    hbm = pl.BlockSpec(memory_space=pl.ANY)
    dma = pltpu.SemaphoreType.DMA
    rows = pl.pallas_call(
        mix_rows,
        name="mix_rows",
        out_shape=jax.ShapeDtypeStruct((8, 2, 512, 256), BF16),
        in_specs=[hbm, vmem, pl.BlockSpec(memory_space=pltpu.SMEM), vmem, hbm],
        out_specs=hbm,
        scratch_shapes=[
            pltpu.VMEM((8, 1024, 128), F32),
            pltpu.VMEM((1024, 1024), BF16),
            pltpu.VMEM((1024, 1024), BF16),
            pltpu.VMEM((1024, 1024), BF16),
            pltpu.VMEM((1024, 1024), BF16),
            pltpu.VMEM((16, 256, 1024), BF16),
            pltpu.VMEM((1024, 512), BF16),
            pltpu.VMEM((4, 256, 128), F32),
            pltpu.VMEM((8, 2, 512, 256), BF16),
            dma((8,)), dma, dma, dma, dma, dma, dma((16,)),
            dma, dma((16,)), dma, dma((16,)), dma((16,)),
        ],
        compiler_params=pltpu.CompilerParams(
            collective_id=0, has_side_effects=True, vmem_limit_bytes=56 << 20),
        cost_estimate=pl.CostEstimate(flops=8 << 30, bytes_accessed=16 << 20, transcendentals=0),
    )(cube.reshape(1024, 1024), residual_op, taper_x.reshape(1, 128), taper_y.reshape(1, 1024), jnp.asarray(row_tables()))
    return pl.pallas_call(
        columns,
        name="columns",
        grid=(8,),
        out_shape=jax.ShapeDtypeStruct((2, 8, 512, 256), BF16),
        in_specs=[pl.BlockSpec((1024, 1024), lambda ch: (0, 0)), pl.BlockSpec((1, 1024, 256), lambda ch: (ch, 0, 0))],
        out_specs=pl.BlockSpec((2, 1, 512, 256), lambda ch: (0, ch, 0, 0)),
        compiler_params=pltpu.CompilerParams(vmem_limit_bytes=32 << 20),
        cost_estimate=pl.CostEstimate(flops=4 << 30, bytes_accessed=10 << 20, transcendentals=0),
    )(jnp.asarray(column_table()), rows.reshape(8, 1024, 256))


def solution(mesh):
    placed = (P("chan", "tile", None), P(), P("tile"), P())
    return jax.shard_map(
        shards, mesh=mesh, in_specs=placed, out_specs=P(None, "chan", None, "tile"), check_vma=False
    )
```

```python
import functools
import math

import jax
import jax.numpy as jnp
import ml_dtypes
import numpy as np
from jax import lax
from jax.experimental import pallas as pl
from jax.experimental.pallas import tpu as pltpu
from jax.sharding import PartitionSpec as P

MESH = pl.DeviceIdType.MESH
BF16 = jnp.bfloat16
F32 = jnp.float32
NX, NY = 512, 1024
PEERS = 63 + 32 + 2
LAG = 5
EARLY = 8
GROUP = 4


def tables(count):
    index = np.arange(count, dtype=np.int64)
    angle = 2.0 * math.pi / count * ((index[:, None] * index[None, :]) % count)
    scale = 1.0 / math.sqrt(count)
    return (np.cos(angle) * scale).astype(np.float32), (-np.sin(angle) * scale).astype(np.float32)


def row_tables():
    cos_y, msin_y = tables(NY)
    parts = [np.concatenate([cos_y[:, 256 * t:256 * t + 256], msin_y[:, 256 * t:256 * t + 256]], 1) for t in range(4)]
    return np.stack(parts).astype(ml_dtypes.bfloat16)


def column_table():
    cos_x, msin_x = tables(NX)
    par, tile, zh, r, cx, cy = np.meshgrid(*[np.arange(n) for n in (2, 4, 4, 2, 4, 2)], indexing="ij")
    order = (tile * 128 + r * 64 + cx * 16 + zh * 4 + 2 * cy + par).reshape(2, 256)
    halves = []
    for some in order:
        cos_s, msin_s = cos_x[:256, some], msin_x[:256, some]
        halves.append(np.concatenate([np.concatenate([cos_s, -msin_s], 1), np.concatenate([msin_s, cos_s], 1)], 0))
    return np.stack(halves).astype(ml_dtypes.bfloat16)


def mix_rows(cube, op, taper_x, taper_y, ytab, rows_out,
             op_here, held, sent, mixed_in, op2, tapered, land, table, wide, rows,
             cube_sem, table_sem, op_sem, out_sem, send1, recv1, send2, land_sem,
             send_fwd, fwd_sem, send_sib, sib_sem, sibf_sem):
    c = lax.axis_index("chan")
    t = lax.axis_index("tile")
    x, j, y = c // 16, (c // 4) % 4, c % 4
    zl, co = t // 2, t % 2
    u = 1 - 2 * zl
    partner = (c, (1 - zl) * 2 + co)
    sibling = (c, zl * 2 + 1 - co)

    loads = [pltpu.make_async_copy(cube.at[:, pl.ds(128 * k, 128)], held.at[k], cube_sem.at[k]) for k in range(8)]
    for load in loads:
        load.start()
    barrier = pltpu.get_barrier_semaphore()

    def greet(d, _):
        pl.semaphore_signal(barrier, inc=1, device_id=(d, t), device_id_type=MESH)
        return 0

    lax.fori_loop(0, c, greet, 0)
    lax.fori_loop(c + 1, 64, greet, 0)
    near, far = (j - u + 4) % 4, (j + 2) % 4
    across = (1 - zl) * 2 + co
    for cx in range(4):
        def greet_far(cy, _, cx=cx):
            for zh in (near, far):
                pl.semaphore_signal(barrier, inc=1, device_id=(cx * 16 + zh * 4 + cy, across), device_id_type=MESH)
            return 0

        lax.fori_loop(0, 4, greet_far, 0)
    for other in (partner, sibling):
        pl.semaphore_signal(barrier, inc=1, device_id=other, device_id_type=MESH)

    halves = (slice(0, 512), slice(512, 1024))
    mine = pl.ds(pl.multiple_of(c * 16, 16), 16)

    def cast(d, half):
        rows_d = pl.ds(pl.multiple_of(d * 16, 16), 16)
        for k in range(4 * half, 4 * half + 4):
            sent[rows_d, 128 * k:128 * k + 128] = held[k, pl.ds(d, 16, stride=64), :].astype(BF16)
        return sent.at[rows_d, halves[half]]

    for half in range(2):
        for load in loads[4 * half:4 * half + 4]:
            load.wait()
        if half == 0:
            pl.semaphore_wait(barrier, PEERS)
        to = mixed_in.at[mine, halves[half]]

        def scatter(k, _, half=half, to=to):
            d = (c + 21 * k) % 64
            pltpu.make_async_remote_copy(
                src_ref=cast(d, half), dst_ref=to, send_sem=send1, recv_sem=recv1.at[half],
                device_id=(d, t), device_id_type=MESH).start()
            return 0

        lax.fori_loop(1, 64, scatter, 0)
        own1 = pltpu.make_async_copy(cast(c, half), to, recv1.at[half])
        own1.start()

    table_load = pltpu.make_async_copy(ytab.at[t], table, table_sem)
    table_load.start()
    op_load = pltpu.make_async_copy(op, op_here, op_sem)
    op_load.start()

    c2 = lax.broadcasted_iota(jnp.int32, (512, 1024), 0)
    spread_k = jnp.where(lax.broadcasted_iota(jnp.int32, (512, 1024), 1) // 2 == c2, 1.0, 0.0).astype(BF16)
    i = lax.broadcasted_iota(jnp.int32, (256, 512), 0)
    cc = lax.broadcasted_iota(jnp.int32, (256, 512), 1)
    same = (lax.broadcasted_iota(jnp.int32, (256, 1024), 0) % 2) == (lax.broadcasted_iota(jnp.int32, (256, 1024), 1) % 2)
    op_load.wait()
    op_low = op_here[...].astype(BF16)

    def expand(zh, _):
        pick = jnp.where((i // 64) * 128 + zh * 32 + (i % 64) // 2 == cc, 1.0, 0.0).astype(BF16)
        some = jnp.dot(pick, op_low, preferred_element_type=F32).astype(BF16)
        full = jnp.dot(some, spread_k, preferred_element_type=F32)
        op2[pl.ds(pl.multiple_of(zh * 256, 256), 256), :] = jnp.where(same, full, 0.0).astype(BF16)
        return 0

    lax.fori_loop(0, 4, expand, 0)
    odd = lax.broadcasted_iota(jnp.int32, (256, 256), 0) % 2 == 1
    tx = jnp.where(odd, taper_x[0, c + 64], taper_x[0, c])
    table_load.wait()

    def mix(st, half):
        delta = jnp.where(st == 0, 0, jnp.where(st == 1, -u, jnp.where(st == 2, u, 2)))
        zh = (j + delta + 4) % 4
        start = pl.multiple_of(zh * 256, 256)
        for n in range(2):
            cols = slice(512 * half + 256 * n, 512 * half + 256 * n + 256)
            part = jnp.dot(op2[pl.ds(start, 256), :], mixed_in[:, cols], preferred_element_type=F32)
            tapered[pl.ds(start, 256), cols] = (part * tx * taper_y[:, cols]).astype(BF16)
        return zh, start

    here = pl.ds(pl.multiple_of(x * 64 + y * 16, 16), 16)

    def send_rows(st, half, k, zh, start):
        to_tile = jnp.where(st % 2 == 1, across, t)
        dx = (x + k // 4) % 4
        dy = (y + k % 4) % 4
        pltpu.make_async_remote_copy(
            src_ref=tapered.at[pl.ds(pl.multiple_of(start + dx * 64 + dy * 16, 16), 16), halves[half]],
            dst_ref=land.at[t * 4 + j, here, halves[half]], send_sem=send2,
            recv_sem=land_sem.at[half * 16 + st * 4 + k // 4],
            device_id=(dx * 16 + zh * 4 + dy, to_tile), device_id_type=MESH).start()

    def mix_half(half):
        pltpu.make_async_copy(sent.at[:, halves[half]], mixed_in.at[:, halves[half]], recv1.at[half]).wait()
        zh2, start2 = mix(2, half)
        zh0, start0 = mix(0, half)
        send_rows(2, half, 0, zh2, start2)
        own2 = pltpu.make_async_copy(
            tapered.at[pl.ds(pl.multiple_of(start0 + x * 64 + y * 16, 16), 16), halves[half]],
            land.at[t * 4 + j, here, halves[half]], land_sem.at[half * 16])
        own2.start()

        def both(k, _):
            send_rows(2, half, k, zh2, start2)
            send_rows(0, half, k, zh0, start0)
            return 0

        lax.fori_loop(1, 16, both, 0)

        def alone(n, _):
            st = 2 * n + 1
            zh, start = mix(st, half)

            def one(k, _):
                send_rows(st, half, k, zh, start)
                return 0

            lax.fori_loop(0, 16, one, 0)
            return 0

        lax.fori_loop(0, 2, alone, 0)

    def group_of(st, passed, other_core):
        z = zl + passed - 2 * zl * passed
        v = 1 - 2 * z
        h = (z + st) % 2
        zh = (j - jnp.where(st == 0, 0, jnp.where(st == 3, 2, v)) + 4) % 4
        core = co + other_core - 2 * co * other_core
        return (h * 2 + core) * 4 + zh

    def piece(st, e, passed, other_core, half=None):
        xs = (x - e + 4) % 4
        cols = slice(None) if half is None else halves[half]
        return land.at[group_of(st, passed, other_core), pl.ds(pl.multiple_of(xs * 64, 64), 64), cols]

    def arrived(ref, sem):
        pltpu.make_async_copy(ref, ref, sem).wait()

    def pass_on(ref, send, recv, device):
        pltpu.make_async_remote_copy(src_ref=ref, dst_ref=ref, send_sem=send, recv_sem=recv,
                                     device_id=device, device_id_type=MESH).start()

    def place(m):
        st = jnp.where(m < 8, 2 * (m % 2), jnp.where(m < 12, 1, 3))
        return st, jnp.where(m < 8, m // 2, m % 4)

    def take_landed(half, m):
        st, e = place(m)
        ref = piece(st, e, 0, 0, half)
        n = st * 4 + e
        arrived(ref, land_sem.at[half * 16 + n])
        pass_on(ref, send_fwd, fwd_sem.at[half * 16 + n], partner)
        pass_on(ref, send_sib, sib_sem.at[n], sibling)

    def take_passed(half, m):
        st, e = place(m)
        ref = piece(st, e, 1, 0, half)
        n = st * 4 + e
        arrived(ref, fwd_sem.at[half * 16 + n])
        pass_on(ref, send_sib, sibf_sem.at[n], sibling)

    def take_sibling(st, passed, sem):
        for e in range(4):
            arrived(piece(st, e, passed, 1), sem.at[st * 4 + e])

    def transform(g):
        for n in range(2):
            part = jnp.dot(land[g], table[:, 256 * n:256 * n + 256], preferred_element_type=F32)
            wide[2 * n] = part[:, :128]
            wide[2 * n + 1] = part[:, 128:]
        span = pl.ds(pl.multiple_of(g * 16, 16), 16)
        for ch in range(8):
            for par in range(2):
                for n in range(4):
                    two = [wide[n, pl.ds(2 * ch + r + 16 * par, 8, stride=32), :] for r in range(2)]
                    at = 256 * ch + 128 * (n % 2)
                    rows[par, n // 2, span, at:at + 128] = jnp.concatenate(two).astype(BF16)
        pltpu.make_async_copy(rows.at[:, :, span], rows_out.at[:, :, span], out_sem).start()

    mix_half(0)

    def landed0(m, _):
        take_landed(0, m)
        return 0

    def step0(m, _):
        take_landed(0, m)
        take_passed(0, m - LAG)
        return 0

    def step1(m, _):
        take_landed(1, m)
        take_passed(1, m - LAG)
        return 0

    lax.fori_loop(0, LAG, landed0, 0)
    lax.fori_loop(LAG, EARLY, step0, 0)
    mix_half(1)
    lax.fori_loop(max(LAG, EARLY), 16, step0, 0)

    def late(m, _):
        take_landed(1, m)
        take_passed(0, 16 - LAG + m)
        return 0

    lax.fori_loop(0, LAG, late, 0)
    lax.fori_loop(LAG, 8, step1, 0)

    waiting = []
    for m in range(8, 16 + LAG):
        if m < 16:
            take_landed(1, m)
        take_passed(1, m - LAG)
        for done, passed in ((m, 0), (m - LAG, 1)):
            for st, at in ((0, 8), (2, 8), (1, 11), (3, 15)):
                if done == at:
                    waiting += [(st, passed, 0), (st, passed, 1)]
        last = m == 15 + LAG
        for _ in range(len(waiting) if last else min(2, len(waiting))):
            st, passed, other_core = waiting.pop(0)
            if other_core:
                take_sibling(st, passed, sibf_sem if passed else sib_sem)
            transform(group_of(st, passed, other_core))

    pltpu.make_async_copy(rows, rows_out, out_sem).wait()
    less = pl.ds(0, 63 * 16)
    pltpu.make_async_copy(sent.at[less], mixed_in.at[less], send1).wait()
    pltpu.make_async_copy(tapered.at[less], tapered.at[less], send2).wait()
    pltpu.make_async_copy(land.at[pl.ds(0, 4)], land.at[pl.ds(0, 4)], send_fwd).wait()
    pltpu.make_async_copy(land.at[pl.ds(0, 8)], land.at[pl.ds(0, 8)], send_sib).wait()


def columns(table, rows, out, table_here, rows_here, out_here, table_sem, rows_sem, out_sem):
    width = 256 * GROUP
    cols = [slice(width * q, width * q + width) for q in range(8 // GROUP)]
    loads = [pltpu.make_async_copy(table, table_here, table_sem)]
    loads += [pltpu.make_async_copy(rows.at[:, :, some], rows_here.at[:, :, some], rows_sem.at[q]) for q, some in enumerate(cols)]
    for load in loads:
        load.start()
    loads[0].wait()
    stores = []
    for q, some in enumerate(cols):
        loads[1 + q].wait()
        chans = slice(GROUP * q, GROUP * q + GROUP)
        for part in range(2):
            span = slice(256 * part, 256 * part + 256)
            even = jnp.dot(table_here[0, span], rows_here[0, :, some], preferred_element_type=F32)
            odd = jnp.dot(table_here[1, span], rows_here[1, :, some], preferred_element_type=F32)
            plus, minus = (even + odd).astype(BF16), (even - odd).astype(BF16)
            for n in range(GROUP):
                out_here[part, GROUP * q + n, :256] = plus[:, 256 * n:256 * n + 256]
                out_here[part, GROUP * q + n, 256:] = minus[:, 256 * n:256 * n + 256]
            store = pltpu.make_async_copy(out_here.at[part, chans], out.at[part, chans], out_sem.at[part, q])
            store.start()
            stores.append(store)
    for store in stores:
        store.wait()


def shards(cube, residual_op, taper_x, taper_y):
    vmem = pl.BlockSpec(memory_space=pltpu.VMEM)
    hbm = pl.BlockSpec(memory_space=pl.ANY)
    dma = pltpu.SemaphoreType.DMA
    rows = pl.pallas_call(
        mix_rows,
        name="mix_rows",
        out_shape=jax.ShapeDtypeStruct((2, 2, 256, 2048), BF16),
        in_specs=[hbm, hbm, pl.BlockSpec(memory_space=pltpu.SMEM), vmem, hbm],
        out_specs=hbm,
        scratch_shapes=[
            pltpu.VMEM((512, 512), F32),
            pltpu.VMEM((8, 1024, 128), F32),
            pltpu.VMEM((1024, 1024), BF16),
            pltpu.VMEM((1024, 1024), BF16),
            pltpu.VMEM((1024, 1024), BF16),
            pltpu.VMEM((1024, 1024), BF16),
            pltpu.VMEM((16, 256, 1024), BF16),
            pltpu.VMEM((1024, 512), BF16),
            pltpu.VMEM((4, 256, 128), F32),
            pltpu.VMEM((2, 2, 256, 2048), BF16),
            dma((8,)), dma, dma, dma, dma, dma((2,)), dma, dma((32,)),
            dma, dma((32,)), dma, dma((16,)), dma((16,)),
        ],
        compiler_params=pltpu.CompilerParams(
            collective_id=0, has_side_effects=True, vmem_limit_bytes=56 << 20),
        cost_estimate=pl.CostEstimate(flops=8 << 30, bytes_accessed=16 << 20, transcendentals=0),
    )(cube.reshape(1024, 1024), residual_op, taper_x.reshape(1, 128), taper_y.reshape(1, 1024), jnp.asarray(row_tables()))
    return pl.pallas_call(
        columns,
        name="columns",
        out_shape=jax.ShapeDtypeStruct((2, 8, 512, 256), BF16),
        in_specs=[hbm, hbm],
        out_specs=hbm,
        scratch_shapes=[
            pltpu.VMEM((2, 512, 512), BF16),
            pltpu.VMEM((2, 512, 2048), BF16),
            pltpu.VMEM((2, 8, 512, 256), BF16),
            dma, dma((8,)), dma((2, 8)),
        ],
        compiler_params=pltpu.CompilerParams(vmem_limit_bytes=60 << 20),
        cost_estimate=pl.CostEstimate(flops=4 << 30, bytes_accessed=10 << 20, transcendentals=0),
    )(jnp.asarray(column_table()), rows.reshape(2, 512, 2048))


def solution(mesh):
    placed = (P("chan", "tile", None), P(), P("tile"), P())
    return jax.shard_map(
        shards, mesh=mesh, in_specs=placed, out_specs=P(None, "chan", None, "tile"), check_vma=False
    )
```

```python
import functools
import math

import jax
import jax.numpy as jnp
import ml_dtypes
import numpy as np
from jax import lax
from jax.experimental import pallas as pl
from jax.experimental.pallas import tpu as pltpu
from jax.sharding import PartitionSpec as P

MESH = pl.DeviceIdType.MESH
BF16 = jnp.bfloat16
F32 = jnp.float32
NX, NY = 512, 1024
PEERS = 63 + 32 + 2
LAG = 5
EARLY = 8
GROUP = 2


def tables(count):
    index = np.arange(count, dtype=np.int64)
    angle = 2.0 * math.pi / count * ((index[:, None] * index[None, :]) % count)
    scale = 1.0 / math.sqrt(count)
    return (np.cos(angle) * scale).astype(np.float32), (-np.sin(angle) * scale).astype(np.float32)


def row_tables():
    cos_y, msin_y = tables(NY)
    parts = [np.concatenate([cos_y[:, 256 * t:256 * t + 256], msin_y[:, 256 * t:256 * t + 256]], 1) for t in range(4)]
    return np.stack(parts).astype(ml_dtypes.bfloat16)


def column_table():
    cos_x, msin_x = tables(NX)
    par, tile, zh, r, cx, cy = np.meshgrid(*[np.arange(n) for n in (2, 4, 4, 2, 4, 2)], indexing="ij")
    order = (tile * 128 + r * 64 + cx * 16 + zh * 4 + 2 * cy + par).reshape(2, 256)
    halves = []
    for some in order:
        cos_s, msin_s = cos_x[:256, some], msin_x[:256, some]
        halves.append(np.concatenate([np.concatenate([cos_s, -msin_s], 1), np.concatenate([msin_s, cos_s], 1)], 0))
    return np.stack(halves).astype(ml_dtypes.bfloat16)


def mix_rows(cube, op, taper_x, taper_y, ytab, xtab, rows, xtab_here,
             tx_here, ty_here, op_here, held, sent, mixed_in, op2, tapered, land, table, wide,
             cube_sem, table_sem, op_sem, xtab_sem, taper_sem, send1, recv1, send2, land_sem,
             send_fwd, fwd_sem, send_sib, sib_sem, sibf_sem):
    c = lax.axis_index("chan")
    t = lax.axis_index("tile")
    x, j, y = c // 16, (c // 4) % 4, c % 4
    zl, co = t // 2, t % 2
    u = 1 - 2 * zl
    partner = (c, (1 - zl) * 2 + co)
    sibling = (c, zl * 2 + 1 - co)

    loads = [pltpu.make_async_copy(cube.at[:, pl.ds(128 * k, 128)], held.at[k], cube_sem.at[k]) for k in range(8)]
    for load in loads:
        load.start()
    barrier = pltpu.get_barrier_semaphore()

    def greet(d, _):
        pl.semaphore_signal(barrier, inc=1, device_id=(d, t), device_id_type=MESH)
        return 0

    lax.fori_loop(0, c, greet, 0)
    lax.fori_loop(c + 1, 64, greet, 0)
    near, far = (j - u + 4) % 4, (j + 2) % 4
    across = (1 - zl) * 2 + co
    for cx in range(4):
        def greet_far(cy, _, cx=cx):
            for zh in (near, far):
                pl.semaphore_signal(barrier, inc=1, device_id=(cx * 16 + zh * 4 + cy, across), device_id_type=MESH)
            return 0

        lax.fori_loop(0, 4, greet_far, 0)
    for other in (partner, sibling):
        pl.semaphore_signal(barrier, inc=1, device_id=other, device_id_type=MESH)

    halves = (slice(0, 512), slice(512, 1024))
    mine = pl.ds(pl.multiple_of(c * 16, 16), 16)

    def cast(d, half):
        rows_d = pl.ds(pl.multiple_of(d * 16, 16), 16)
        for k in range(4 * half, 4 * half + 4):
            sent[rows_d, 128 * k:128 * k + 128] = held[k, pl.ds(d, 16, stride=64), :].astype(BF16)
        return sent.at[rows_d, halves[half]]

    for half in range(2):
        for load in loads[4 * half:4 * half + 4]:
            load.wait()
        if half == 0:
            pl.semaphore_wait(barrier, PEERS)
        to = mixed_in.at[mine, halves[half]]

        def scatter(k, _, half=half, to=to):
            d = (c + 21 * k) % 64
            pltpu.make_async_remote_copy(
                src_ref=cast(d, half), dst_ref=to, send_sem=send1, recv_sem=recv1.at[half],
                device_id=(d, t), device_id_type=MESH).start()
            return 0

        lax.fori_loop(1, 64, scatter, 0)
        own1 = pltpu.make_async_copy(cast(c, half), to, recv1.at[half])
        own1.start()

    table_load = pltpu.make_async_copy(ytab.at[t], table, table_sem)
    table_load.start()
    op_load = pltpu.make_async_copy(op, op_here, op_sem)
    op_load.start()
    xtab_load = pltpu.make_async_copy(xtab, xtab_here, xtab_sem)
    xtab_load.start()
    taper_loads = [pltpu.make_async_copy(taper_x, tx_here, taper_sem.at[0]),
                   pltpu.make_async_copy(taper_y, ty_here, taper_sem.at[1])]
    for load in taper_loads:
        load.start()

    c2 = lax.broadcasted_iota(jnp.int32, (512, 1024), 0)
    spread_k = jnp.where(lax.broadcasted_iota(jnp.int32, (512, 1024), 1) // 2 == c2, 1.0, 0.0).astype(BF16)
    i = lax.broadcasted_iota(jnp.int32, (256, 512), 0)
    cc = lax.broadcasted_iota(jnp.int32, (256, 512), 1)
    same = (lax.broadcasted_iota(jnp.int32, (256, 1024), 0) % 2) == (lax.broadcasted_iota(jnp.int32, (256, 1024), 1) % 2)
    op_load.wait()
    op_low = op_here[...].astype(BF16)

    def expand(zh, _):
        pick = jnp.where((i // 64) * 128 + zh * 32 + (i % 64) // 2 == cc, 1.0, 0.0).astype(BF16)
        some = jnp.dot(pick, op_low, preferred_element_type=F32).astype(BF16)
        full = jnp.dot(some, spread_k, preferred_element_type=F32)
        op2[pl.ds(pl.multiple_of(zh * 256, 256), 256), :] = jnp.where(same, full, 0.0).astype(BF16)
        return 0

    lax.fori_loop(0, 4, expand, 0)
    odd = lax.broadcasted_iota(jnp.int32, (256, 256), 0) % 2 == 1
    for load in taper_loads:
        load.wait()
    tx = jnp.where(odd, tx_here[0, c + 64], tx_here[0, c])
    table_load.wait()

    def mix(st, half):
        delta = jnp.where(st == 0, 0, jnp.where(st == 1, -u, jnp.where(st == 2, u, 2)))
        zh = (j + delta + 4) % 4
        start = pl.multiple_of(zh * 256, 256)
        for n in range(2):
            cols = slice(512 * half + 256 * n, 512 * half + 256 * n + 256)
            part = jnp.dot(op2[pl.ds(start, 256), :], mixed_in[:, cols], preferred_element_type=F32)
            tapered[pl.ds(start, 256), cols] = (part * tx * ty_here[:, cols]).astype(BF16)
        return zh, start

    here = pl.ds(pl.multiple_of(x * 64 + y * 16, 16), 16)

    def send_rows(st, half, k, zh, start):
        to_tile = jnp.where(st % 2 == 1, across, t)
        dx = (x + k // 4) % 4
        dy = (y + k % 4) % 4
        pltpu.make_async_remote_copy(
            src_ref=tapered.at[pl.ds(pl.multiple_of(start + dx * 64 + dy * 16, 16), 16), halves[half]],
            dst_ref=land.at[t * 4 + j, here, halves[half]], send_sem=send2,
            recv_sem=land_sem.at[half * 16 + st * 4 + k // 4],
            device_id=(dx * 16 + zh * 4 + dy, to_tile), device_id_type=MESH).start()

    def mix_half(half):
        pltpu.make_async_copy(sent.at[:, halves[half]], mixed_in.at[:, halves[half]], recv1.at[half]).wait()
        zh2, start2 = mix(2, half)
        zh0, start0 = mix(0, half)
        send_rows(2, half, 0, zh2, start2)
        own2 = pltpu.make_async_copy(
            tapered.at[pl.ds(pl.multiple_of(start0 + x * 64 + y * 16, 16), 16), halves[half]],
            land.at[t * 4 + j, here, halves[half]], land_sem.at[half * 16])
        own2.start()

        def both(k, _):
            send_rows(2, half, k, zh2, start2)
            send_rows(0, half, k, zh0, start0)
            return 0

        lax.fori_loop(1, 16, both, 0)

        def alone(n, _):
            st = 2 * n + 1
            zh, start = mix(st, half)

            def one(k, _):
                send_rows(st, half, k, zh, start)
                return 0

            lax.fori_loop(0, 16, one, 0)
            return 0

        lax.fori_loop(0, 2, alone, 0)

    def group_of(st, passed, other_core):
        z = zl + passed - 2 * zl * passed
        v = 1 - 2 * z
        h = (z + st) % 2
        zh = (j - jnp.where(st == 0, 0, jnp.where(st == 3, 2, v)) + 4) % 4
        core = co + other_core - 2 * co * other_core
        return (h * 2 + core) * 4 + zh

    def piece(st, e, passed, other_core, half=None):
        xs = (x - e + 4) % 4
        cols = slice(None) if half is None else halves[half]
        return land.at[group_of(st, passed, other_core), pl.ds(pl.multiple_of(xs * 64, 64), 64), cols]

    def arrived(ref, sem):
        pltpu.make_async_copy(ref, ref, sem).wait()

    def pass_on(ref, send, recv, device):
        pltpu.make_async_remote_copy(src_ref=ref, dst_ref=ref, send_sem=send, recv_sem=recv,
                                     device_id=device, device_id_type=MESH).start()

    def place(m):
        st = jnp.where(m < 8, 2 * (m % 2), jnp.where(m < 12, 1, 3))
        return st, jnp.where(m < 8, m // 2, m % 4)

    def take_landed(half, m):
        st, e = place(m)
        ref = piece(st, e, 0, 0, half)
        n = st * 4 + e
        arrived(ref, land_sem.at[half * 16 + n])
        pass_on(ref, send_fwd, fwd_sem.at[half * 16 + n], partner)
        pass_on(ref, send_sib, sib_sem.at[n], sibling)

    def take_passed(half, m):
        st, e = place(m)
        ref = piece(st, e, 1, 0, half)
        n = st * 4 + e
        arrived(ref, fwd_sem.at[half * 16 + n])
        pass_on(ref, send_sib, sibf_sem.at[n], sibling)

    def take_sibling(st, passed, sem):
        for e in range(4):
            arrived(piece(st, e, passed, 1), sem.at[st * 4 + e])

    def transform(g):
        for n in range(2):
            part = jnp.dot(land[g], table[:, 256 * n:256 * n + 256], preferred_element_type=F32)
            wide[2 * n] = part[:, :128]
            wide[2 * n + 1] = part[:, 128:]
        spans = [pl.ds(pl.multiple_of(256 * part + g * 16, 16), 16) for part in range(2)]
        for ch in range(8):
            for par in range(2):
                for n in range(4):
                    two = [wide[n, pl.ds(2 * ch + r + 16 * par, 8, stride=32), :] for r in range(2)]
                    at = 256 * ch + 128 * (n % 2)
                    rows[par, spans[n // 2], at:at + 128] = jnp.concatenate(two).astype(BF16)

    mix_half(0)

    def landed0(m, _):
        take_landed(0, m)
        return 0

    def step0(m, _):
        take_landed(0, m)
        take_passed(0, m - LAG)
        return 0

    def step1(m, _):
        take_landed(1, m)
        take_passed(1, m - LAG)
        return 0

    lax.fori_loop(0, LAG, landed0, 0)
    lax.fori_loop(LAG, EARLY, step0, 0)
    mix_half(1)
    lax.fori_loop(max(LAG, EARLY), 16, step0, 0)

    def late(m, _):
        take_landed(1, m)
        take_passed(0, 16 - LAG + m)
        return 0

    lax.fori_loop(0, LAG, late, 0)
    lax.fori_loop(LAG, 8, step1, 0)

    waiting = []
    for m in range(8, 16 + LAG):
        if m < 16:
            take_landed(1, m)
        take_passed(1, m - LAG)
        for done, passed in ((m, 0), (m - LAG, 1)):
            for st, at in ((0, 8), (2, 8), (1, 11), (3, 15)):
                if done == at:
                    waiting += [(st, passed, 0), (st, passed, 1)]
        last = m == 15 + LAG
        for _ in range(len(waiting) if last else min(2, len(waiting))):
            st, passed, other_core = waiting.pop(0)
            if other_core:
                take_sibling(st, passed, sibf_sem if passed else sib_sem)
            transform(group_of(st, passed, other_core))

    xtab_load.wait()
    less = pl.ds(0, 63 * 16)
    pltpu.make_async_copy(sent.at[less], mixed_in.at[less], send1).wait()
    pltpu.make_async_copy(tapered.at[less], tapered.at[less], send2).wait()
    pltpu.make_async_copy(land.at[pl.ds(0, 4)], land.at[pl.ds(0, 4)], send_fwd).wait()
    pltpu.make_async_copy(land.at[pl.ds(0, 8)], land.at[pl.ds(0, 8)], send_sib).wait()


def columns(table, rows, out, out_here, out_sem):
    stores = []
    for q in range(8 // GROUP):
        some = slice(256 * GROUP * q, 256 * GROUP * (q + 1))
        chans = slice(GROUP * q, GROUP * q + GROUP)
        for part in range(2):
            span = slice(256 * part, 256 * part + 256)
            even = jnp.dot(table[0, span], rows[0, :, some], preferred_element_type=F32)
            odd = jnp.dot(table[1, span], rows[1, :, some], preferred_element_type=F32)
            plus, minus = (even + odd).astype(BF16), (even - odd).astype(BF16)
            for n in range(GROUP):
                out_here[part, GROUP * q + n, :256] = plus[:, 256 * n:256 * n + 256]
                out_here[part, GROUP * q + n, 256:] = minus[:, 256 * n:256 * n + 256]
            store = pltpu.make_async_copy(out_here.at[part, chans], out.at[part, chans], out_sem.at[part, q])
            store.start()
            stores.append(store)
    for store in stores:
        store.wait()


def shards(cube, residual_op, taper_x, taper_y):
    vmem = pl.BlockSpec(memory_space=pltpu.VMEM)
    hbm = pl.BlockSpec(memory_space=pl.ANY)
    dma = pltpu.SemaphoreType.DMA

    def in_hbm(array):
        return pltpu.with_memory_space_constraint(array, pltpu.HBM)

    def in_vmem(array):
        return pltpu.with_memory_space_constraint(array, pltpu.VMEM)

    rows, xtab = pl.pallas_call(
        mix_rows,
        name="mix_rows",
        out_shape=[pltpu.VMEM((2, 512, 2048), BF16), pltpu.VMEM((2, 512, 512), BF16)],
        in_specs=[hbm] * 6,
        out_specs=[vmem, vmem],
        scratch_shapes=[
            pltpu.SMEM((1, 128), F32),
            pltpu.VMEM((1, 1024), F32),
            pltpu.VMEM((512, 512), F32),
            pltpu.VMEM((8, 1024, 128), F32),
            pltpu.VMEM((1024, 1024), BF16),
            pltpu.VMEM((1024, 1024), BF16),
            pltpu.VMEM((1024, 1024), BF16),
            pltpu.VMEM((1024, 1024), BF16),
            pltpu.VMEM((16, 256, 1024), BF16),
            pltpu.VMEM((1024, 512), BF16),
            pltpu.VMEM((4, 256, 128), F32),
            dma((8,)), dma, dma, dma, dma((2,)), dma, dma((2,)), dma, dma((32,)),
            dma, dma((32,)), dma, dma((16,)), dma((16,)),
        ],
        compiler_params=pltpu.CompilerParams(
            collective_id=0, has_side_effects=True, vmem_limit_bytes=38 << 20),
        cost_estimate=pl.CostEstimate(flops=8 << 30, bytes_accessed=16 << 20, transcendentals=0),
    )(in_hbm(cube.reshape(1024, 1024)), in_hbm(residual_op), in_hbm(taper_x.reshape(1, 128)),
      in_hbm(taper_y.reshape(1, 1024)), in_hbm(jnp.asarray(row_tables())), in_hbm(jnp.asarray(column_table())))
    return pl.pallas_call(
        columns,
        name="columns",
        out_shape=jax.ShapeDtypeStruct((2, 8, 512, 256), BF16),
        in_specs=[vmem, vmem],
        out_specs=hbm,
        scratch_shapes=[pltpu.VMEM((2, 8, 512, 256), BF16), dma((2, 8))],
        compiler_params=pltpu.CompilerParams(vmem_limit_bytes=24 << 20),
        cost_estimate=pl.CostEstimate(flops=4 << 30, bytes_accessed=10 << 20, transcendentals=0),
    )(in_vmem(xtab), in_vmem(rows))


def solution(mesh):
    placed = (P("chan", "tile", None), P(), P("tile"), P())
    return jax.shard_map(
        shards, mesh=mesh, in_specs=placed, out_specs=P(None, "chan", None, "tile"), check_vma=False
    )
```

```python
import functools
import math

import jax
import jax.numpy as jnp
import ml_dtypes
import numpy as np
from jax import lax
from jax.experimental import pallas as pl
from jax.experimental.pallas import tpu as pltpu
from jax.sharding import PartitionSpec as P

MESH = pl.DeviceIdType.MESH
BF16 = jnp.bfloat16
F32 = jnp.float32
NX, NY = 512, 1024
PEERS = 63 + 32 + 2
LAG = 5
EARLY = 8
GROUP = 1


def tables(count):
    index = np.arange(count, dtype=np.int64)
    angle = 2.0 * math.pi / count * ((index[:, None] * index[None, :]) % count)
    scale = 1.0 / math.sqrt(count)
    return (np.cos(angle) * scale).astype(np.float32), (-np.sin(angle) * scale).astype(np.float32)


def row_tables():
    cos_y, msin_y = tables(NY)
    parts = [np.concatenate([cos_y[:, 256 * t:256 * t + 256], msin_y[:, 256 * t:256 * t + 256]], 1) for t in range(4)]
    return np.stack(parts).astype(ml_dtypes.bfloat16)


def column_table():
    cos_x, msin_x = tables(NX)
    par, tile, zh, r, cx, cy = np.meshgrid(*[np.arange(n) for n in (2, 4, 4, 2, 4, 2)], indexing="ij")
    order = (tile * 128 + r * 64 + cx * 16 + zh * 4 + 2 * cy + par).reshape(2, 256)
    halves = []
    for some in order:
        cos_s, msin_s = cos_x[:256, some], msin_x[:256, some]
        halves.append(np.concatenate([np.concatenate([cos_s, -msin_s], 1), np.concatenate([msin_s, cos_s], 1)], 0))
    return np.stack(halves).astype(ml_dtypes.bfloat16)


def mix_rows(cube, op, taper_x, taper_y, ytab, xtab, rows, xtab_here,
             tx_here, ty_here, op_here, held, sent, mixed_in, op2, tapered, land, table, wide,
             cube_sem, table_sem, op_sem, xtab_sem, taper_sem, send1, recv1, send2, land_sem,
             send_fwd, fwd_sem, send_sib, sib_sem, sibf_sem):
    c = lax.axis_index("chan")
    t = lax.axis_index("tile")
    x, j, y = c // 16, (c // 4) % 4, c % 4
    zl, co = t // 2, t % 2
    u = 1 - 2 * zl
    partner = (c, (1 - zl) * 2 + co)
    sibling = (c, zl * 2 + 1 - co)

    loads = [pltpu.make_async_copy(cube.at[:, pl.ds(128 * k, 128)], held.at[k], cube_sem.at[k]) for k in range(8)]
    for load in loads[:4]:
        load.start()
    barrier = pltpu.get_barrier_semaphore()

    def greet(d, _):
        pl.semaphore_signal(barrier, inc=1, device_id=(d, t), device_id_type=MESH)
        return 0

    lax.fori_loop(0, c, greet, 0)
    lax.fori_loop(c + 1, 64, greet, 0)
    near, far = (j - u + 4) % 4, (j + 2) % 4
    across = (1 - zl) * 2 + co
    for cx in range(4):
        def greet_far(cy, _, cx=cx):
            for zh in (near, far):
                pl.semaphore_signal(barrier, inc=1, device_id=(cx * 16 + zh * 4 + cy, across), device_id_type=MESH)
            return 0

        lax.fori_loop(0, 4, greet_far, 0)
    for other in (partner, sibling):
        pl.semaphore_signal(barrier, inc=1, device_id=other, device_id_type=MESH)

    for load in loads[4:]:
        load.start()
    halves = (slice(0, 512), slice(512, 1024))
    mine = pl.ds(pl.multiple_of(c * 16, 16), 16)

    def cast(d, half):
        rows_d = pl.ds(pl.multiple_of(d * 16, 16), 16)
        for k in range(4 * half, 4 * half + 4):
            sent[rows_d, 128 * k:128 * k + 128] = held[k, pl.ds(d, 16, stride=64), :].astype(BF16)
        return sent.at[rows_d, halves[half]]

    for half in range(2):
        for load in loads[4 * half:4 * half + 4]:
            load.wait()
        if half == 0:
            pl.semaphore_wait(barrier, PEERS)
        to = mixed_in.at[mine, halves[half]]

        def scatter(k, _, half=half, to=to):
            d = (c + 21 * k) % 64
            pltpu.make_async_remote_copy(
                src_ref=cast(d, half), dst_ref=to, send_sem=send1, recv_sem=recv1.at[half],
                device_id=(d, t), device_id_type=MESH).start()
            return 0

        lax.fori_loop(1, 64, scatter, 0, unroll=3)
        own1 = pltpu.make_async_copy(cast(c, half), to, recv1.at[half])
        own1.start()

    table_load = pltpu.make_async_copy(ytab.at[t], table, table_sem)
    table_load.start()
    op_load = pltpu.make_async_copy(op, op_here, op_sem)
    op_load.start()
    xtab_load = pltpu.make_async_copy(xtab, xtab_here, xtab_sem)
    xtab_load.start()
    taper_loads = [pltpu.make_async_copy(taper_x, tx_here, taper_sem.at[0]),
                   pltpu.make_async_copy(taper_y, ty_here, taper_sem.at[1])]
    for load in taper_loads:
        load.start()

    c2 = lax.broadcasted_iota(jnp.int32, (512, 1024), 0)
    spread_k = jnp.where(lax.broadcasted_iota(jnp.int32, (512, 1024), 1) // 2 == c2, 1.0, 0.0).astype(BF16)
    i = lax.broadcasted_iota(jnp.int32, (256, 512), 0)
    cc = lax.broadcasted_iota(jnp.int32, (256, 512), 1)
    same = (lax.broadcasted_iota(jnp.int32, (256, 1024), 0) % 2) == (lax.broadcasted_iota(jnp.int32, (256, 1024), 1) % 2)
    op_load.wait()
    op_low = op_here[...].astype(BF16)

    def expand(zh, _):
        pick = jnp.where((i // 64) * 128 + zh * 32 + (i % 64) // 2 == cc, 1.0, 0.0).astype(BF16)
        some = jnp.dot(pick, op_low, preferred_element_type=F32).astype(BF16)
        full = jnp.dot(some, spread_k, preferred_element_type=F32)
        op2[pl.ds(pl.multiple_of(zh * 256, 256), 256), :] = jnp.where(same, full, 0.0).astype(BF16)
        return 0

    lax.fori_loop(0, 4, expand, 0)
    odd = lax.broadcasted_iota(jnp.int32, (256, 256), 0) % 2 == 1
    for load in taper_loads:
        load.wait()
    tx = jnp.where(odd, tx_here[0, c + 64], tx_here[0, c])
    table_load.wait()

    def mix(st, half):
        delta = (0, -u, u, 2)[st]
        zh = (j + delta + 4) % 4
        start = pl.multiple_of(zh * 256, 256)
        for n in range(2):
            cols = slice(512 * half + 256 * n, 512 * half + 256 * n + 256)
            part = jnp.dot(op2[pl.ds(start, 256), :], mixed_in[:, cols], preferred_element_type=F32)
            tapered[pl.ds(start, 256), cols] = (part * tx * ty_here[:, cols]).astype(BF16)
        return zh, start

    here = pl.ds(pl.multiple_of(x * 64 + y * 16, 16), 16)

    slot = t * 4 + j
    dys = [(y + f) % 4 for f in range(4)]

    def send_rows(st, half, e, dx, dy, zh, start):
        to_tile = across if st % 2 == 1 else t
        pltpu.make_async_remote_copy(
            src_ref=tapered.at[pl.ds(pl.multiple_of(start + dx * 64 + dy * 16, 16), 16), halves[half]],
            dst_ref=land.at[slot, here, halves[half]], send_sem=send2, recv_sem=land_sem.at[half * 16 + st * 4 + e],
            device_id=(dx * 16 + zh * 4 + dy, to_tile), device_id_type=MESH).start()

    def mix_half(half):
        pltpu.make_async_copy(sent.at[:, halves[half]], mixed_in.at[:, halves[half]], recv1.at[half]).wait()
        zh2, start2 = mix(2, half)
        zh0, start0 = mix(0, half)
        send_rows(2, half, 0, x, y, zh2, start2)
        own2 = pltpu.make_async_copy(
            tapered.at[pl.ds(pl.multiple_of(start0 + x * 64 + y * 16, 16), 16), halves[half]],
            land.at[slot, here, halves[half]], land_sem.at[half * 16])
        own2.start()
        for dy in dys[1:]:
            send_rows(2, half, 0, x, dy, zh2, start2)
            send_rows(0, half, 0, x, dy, zh0, start0)

        def both(e, _):
            dx = (x + e) % 4
            for dy in dys:
                send_rows(2, half, e, dx, dy, zh2, start2)
                send_rows(0, half, e, dx, dy, zh0, start0)
            return 0

        lax.fori_loop(1, 4, both, 0)
        for st in (1, 3):
            zh, start = mix(st, half)

            def one(e, _, st=st, zh=zh, start=start):
                dx = (x + e) % 4
                for dy in dys:
                    send_rows(st, half, e, dx, dy, zh, start)
                return 0

            lax.fori_loop(0, 4, one, 0)

    def group_of(st, passed, other_core):
        z = zl + passed - 2 * zl * passed
        v = 1 - 2 * z
        h = (z + st) % 2
        zh = (j - jnp.where(st == 0, 0, jnp.where(st == 3, 2, v)) + 4) % 4
        core = co + other_core - 2 * co * other_core
        return (h * 2 + core) * 4 + zh

    def piece(st, e, passed, other_core, half=None):
        xs = (x - e + 4) % 4
        cols = slice(None) if half is None else halves[half]
        return land.at[group_of(st, passed, other_core), pl.ds(pl.multiple_of(xs * 64, 64), 64), cols]

    def arrived(ref, sem):
        pltpu.make_async_copy(ref, ref, sem).wait()

    def pass_on(ref, send, recv, device):
        pltpu.make_async_remote_copy(src_ref=ref, dst_ref=ref, send_sem=send, recv_sem=recv,
                                     device_id=device, device_id_type=MESH).start()

    def place(m):
        st = jnp.where(m < 8, 2 * (m % 2), jnp.where(m < 12, 1, 3))
        return st, jnp.where(m < 8, m // 2, m % 4)

    def take_landed(half, m):
        st, e = place(m)
        ref = piece(st, e, 0, 0, half)
        n = st * 4 + e
        arrived(ref, land_sem.at[half * 16 + n])
        pass_on(ref, send_fwd, fwd_sem.at[half * 16 + n], partner)
        pass_on(ref, send_sib, sib_sem.at[n], sibling)

    def take_passed(half, m):
        st, e = place(m)
        ref = piece(st, e, 1, 0, half)
        n = st * 4 + e
        arrived(ref, fwd_sem.at[half * 16 + n])
        pass_on(ref, send_sib, sibf_sem.at[n], sibling)

    def take_sibling(st, passed, sem):
        for e in range(4):
            arrived(piece(st, e, passed, 1), sem.at[st * 4 + e])

    def transform(g):
        for n in range(2):
            part = jnp.dot(land[g], table[:, 256 * n:256 * n + 256], preferred_element_type=F32)
            wide[2 * n] = part[:, :128]
            wide[2 * n + 1] = part[:, 128:]
        spans = [pl.ds(pl.multiple_of(256 * part + g * 16, 16), 16) for part in range(2)]
        for ch in range(8):
            for par in range(2):
                for n in range(4):
                    two = [wide[n, pl.ds(2 * ch + r + 16 * par, 8, stride=32), :] for r in range(2)]
                    at = 256 * ch + 128 * (n % 2)
                    rows[par, spans[n // 2], at:at + 128] = jnp.concatenate(two).astype(BF16)

    mix_half(0)

    def landed0(m, _):
        take_landed(0, m)
        return 0

    def step0(m, _):
        take_landed(0, m)
        take_passed(0, m - LAG)
        return 0

    def step1(m, _):
        take_landed(1, m)
        take_passed(1, m - LAG)
        return 0

    lax.fori_loop(0, LAG, landed0, 0)
    lax.fori_loop(LAG, EARLY, step0, 0)
    mix_half(1)
    lax.fori_loop(max(LAG, EARLY), 16, step0, 0)

    def late(m, _):
        take_landed(1, m)
        take_passed(0, 16 - LAG + m)
        return 0

    lax.fori_loop(0, LAG, late, 0)
    lax.fori_loop(LAG, 8, step1, 0)

    waiting = []
    for m in range(8, 16 + LAG):
        if m < 16:
            take_landed(1, m)
        take_passed(1, m - LAG)
        for done, passed in ((m, 0), (m - LAG, 1)):
            for st, at in ((0, 8), (2, 8), (1, 11), (3, 15)):
                if done == at:
                    waiting += [(st, passed, 0), (st, passed, 1)]
        last = m == 15 + LAG
        for _ in range(len(waiting) if last else min(2, len(waiting))):
            st, passed, other_core = waiting.pop(0)
            if other_core:
                take_sibling(st, passed, sibf_sem if passed else sib_sem)
            transform(group_of(st, passed, other_core))

    xtab_load.wait()
    less = pl.ds(0, 63 * 16)
    pltpu.make_async_copy(sent.at[less], mixed_in.at[less], send1).wait()
    pltpu.make_async_copy(tapered.at[less], tapered.at[less], send2).wait()
    pltpu.make_async_copy(land.at[pl.ds(0, 4)], land.at[pl.ds(0, 4)], send_fwd).wait()
    pltpu.make_async_copy(land.at[pl.ds(0, 8)], land.at[pl.ds(0, 8)], send_sib).wait()


def columns(table, rows, out, out_here, out_sem):
    stores = []
    for q in range(8 // GROUP):
        some = slice(256 * GROUP * q, 256 * GROUP * (q + 1))
        chans = slice(GROUP * q, GROUP * q + GROUP)
        for part in range(2):
            span = slice(256 * part, 256 * part + 256)
            even = jnp.dot(table[0, span], rows[0, :, some], preferred_element_type=F32)
            odd = jnp.dot(table[1, span], rows[1, :, some], preferred_element_type=F32)
            plus, minus = (even + odd).astype(BF16), (even - odd).astype(BF16)
            for n in range(GROUP):
                out_here[part, GROUP * q + n, :256] = plus[:, 256 * n:256 * n + 256]
                out_here[part, GROUP * q + n, 256:] = minus[:, 256 * n:256 * n + 256]
            store = pltpu.make_async_copy(out_here.at[part, chans], out.at[part, chans], out_sem.at[part, q])
            store.start()
            stores.append(store)
    for store in stores:
        store.wait()


def shards(cube, residual_op, taper_x, taper_y):
    vmem = pl.BlockSpec(memory_space=pltpu.VMEM)
    hbm = pl.BlockSpec(memory_space=pl.ANY)
    dma = pltpu.SemaphoreType.DMA

    def in_hbm(array):
        return pltpu.with_memory_space_constraint(array, pltpu.HBM)

    def in_vmem(array):
        return pltpu.with_memory_space_constraint(array, pltpu.VMEM)

    rows, xtab = pl.pallas_call(
        mix_rows,
        name="mix_rows",
        out_shape=[pltpu.VMEM((2, 512, 2048), BF16), pltpu.VMEM((2, 512, 512), BF16)],
        in_specs=[hbm] * 6,
        out_specs=[vmem, vmem],
        scratch_shapes=[
            pltpu.SMEM((1, 128), F32),
            pltpu.VMEM((1, 1024), F32),
            pltpu.VMEM((512, 512), F32),
            pltpu.VMEM((8, 1024, 128), F32),
            pltpu.VMEM((1024, 1024), BF16),
            pltpu.VMEM((1024, 1024), BF16),
            pltpu.VMEM((1024, 1024), BF16),
            pltpu.VMEM((1024, 1024), BF16),
            pltpu.VMEM((16, 256, 1024), BF16),
            pltpu.VMEM((1024, 512), BF16),
            pltpu.VMEM((4, 256, 128), F32),
            dma((8,)), dma, dma, dma, dma((2,)), dma, dma((2,)), dma, dma((32,)),
            dma, dma((32,)), dma, dma((16,)), dma((16,)),
        ],
        compiler_params=pltpu.CompilerParams(
            collective_id=0, has_side_effects=True, vmem_limit_bytes=38 << 20),
        cost_estimate=pl.CostEstimate(flops=8 << 30, bytes_accessed=16 << 20, transcendentals=0),
    )(in_hbm(cube.reshape(1024, 1024)), in_hbm(residual_op), in_hbm(taper_x.reshape(1, 128)),
      in_hbm(taper_y.reshape(1, 1024)), in_hbm(jnp.asarray(row_tables())), in_hbm(jnp.asarray(column_table())))
    return pl.pallas_call(
        columns,
        name="columns",
        out_shape=jax.ShapeDtypeStruct((2, 8, 512, 256), BF16),
        in_specs=[vmem, vmem],
        out_specs=hbm,
        scratch_shapes=[pltpu.VMEM((2, 8, 512, 256), BF16), dma((2, 8))],
        compiler_params=pltpu.CompilerParams(vmem_limit_bytes=24 << 20),
        cost_estimate=pl.CostEstimate(flops=4 << 30, bytes_accessed=10 << 20, transcendentals=0),
    )(in_vmem(xtab), in_vmem(rows))


def solution(mesh):
    placed = (P("chan", "tile", None), P(), P("tile"), P())
    return jax.shard_map(
        shards, mesh=mesh, in_specs=placed, out_specs=P(None, "chan", None, "tile"), check_vma=False
    )
```
